32 devices in a mesh: ha: 4 (over y, x), wa: 8 (over z, core).
Axes of the slice: x: 2, y: 2, z: 4, core: 2. Of those that a mesh axis runs over, the one named last changes fastest.
Arguments:
- tokens: bfloat16 [4, 32, 64, 1536], P(None, 'ha', 'wa'), may hold values from -6 to 6
- shift: float32 [1536], replicated, may hold values from -3 to 3
- scale: float32 [1536], replicated, may hold values from -3 to 3
- gate: float32 [1536], replicated, may hold values from -4 to 4
- qkv_weight: bfloat16 [1536, 4608], P('wa'), may hold values from -0.17860863 to 0.17860863
- out_weight: bfloat16 [1536, 1536], P('wa'), may hold values from -0.15625 to 0.15625
- q_gain: float32 [128], replicated, may hold values from 1.4 to 6.5
- k_gain: float32 [128], replicated, may hold values from 1.4 to 6.5
Outputs:
- update: bfloat16 [4, 32, 64, 1536], P(None, 'ha', 'wa')
The draws below stay inside these ranges and needn't reach their ends.
All inputs are finite; a program needn't handle non-finite values.
Results may differ from the reference program's by a relative error of at most 0.009.
The reference program's roundings to bfloat16 on the way count: a program that leaves them out, or rounds other values in their place, can miss the bound.
Values may be sent and summed in bfloat16 or wider, within the bound.
A program may use at most 128 MiB of HBM per device.

```python
import jax
import jax.numpy as jnp
from jax import lax

D = 1536
HEADS = 12
HD = 128
TILE_T = 4
TILE_H = 8
TILE_W = 8
INNER = 1536
FRAMES = 4
HEIGHT = 32
WIDTH = 64


def draw_tokens(key, part):
    shape = (FRAMES, HEIGHT, WIDTH, D)
    values = jnp.clip(jax.random.normal(key, shape, jnp.float32), -6.0, 6.0)
    return values.astype(jnp.bfloat16)


def draw_qkv_weight(key, part):
    inner = HEADS * HD
    base = jnp.clip(jax.random.normal(key, (D, 3 * inner), jnp.float32), -5.0, 5.0)
    return (base / jnp.sqrt(jnp.float32(D))).astype(jnp.bfloat16)


def draw_gain(key):
    return jax.random.uniform(key, (HD,), jnp.float32, 1.4, 2.6)


def draw_q_gain(key, part):
    return draw_gain(jax.random.fold_in(key, 11))


def draw_k_gain(key, part):
    return draw_gain(jax.random.fold_in(key, 13))


def block_levels(own_key, dims, split, least, largest):
    def one(position, parts):
        steps = jax.random.uniform(jax.random.fold_in(jax.random.fold_in(own_key, 6), position), (parts,), jnp.float32, least / len(split), largest / len(split))
        return jnp.repeat(jnp.exp(steps), dims[position] // parts).reshape((-1,) + (1,) * (len(dims) - position - 1))

    factor_of = one(*split[0])
    for cut in split[1:]:
        factor_of = factor_of * one(*cut)
    return factor_of


def scatter_about(key, shape, width, most, pieces=(), kind=jnp.bfloat16):
    values = width * jax.random.normal(key, shape, jnp.float32)
    if pieces:
        values = values * block_levels(key, shape, pieces, -0.22, 0.18)
    return jnp.clip(values, -most, most).astype(kind)


def setup_inputs(seed: int = 0) -> dict:
    splits = jax.random.split(jax.random.key(seed), 9)
    tokens = draw_tokens(jax.random.fold_in(splits[8], 71), 0)
    shift = scatter_about(splits[1], (D,), 0.5, 3.0, (), jnp.float32)
    scale = scatter_about(splits[2], (D,), 0.5, 3.0, (), jnp.float32)
    gate = scatter_about(splits[3], (D,), 1.0, 4.0, (), jnp.float32)
    qkv_weight = draw_qkv_weight(jax.random.fold_in(splits[8], 71), 0)
    out_weight = scatter_about(splits[5], (INNER, D), INNER ** -0.5, 0.15625, ((0, 8),))
    q_gain = draw_q_gain(jax.random.fold_in(splits[8], 71), 0)
    k_gain = draw_k_gain(jax.random.fold_in(splits[8], 71), 0)
    return dict(tokens=tokens, shift=shift, scale=scale, gate=gate, qkv_weight=qkv_weight, out_weight=out_weight, q_gain=q_gain, k_gain=k_gain)


def reference(tokens, shift, scale, gate, qkv_weight, out_weight, q_gain, k_gain):
    inner = HEADS * HD
    flat = tokens.reshape(-1, D).astype(jnp.float32)
    mean = lax.optimization_barrier(jnp.mean(flat, axis=-1, keepdims=True))
    centred = flat - mean
    var = lax.optimization_barrier(jnp.mean(centred * centred, axis=-1, keepdims=True))
    normed = centred / jnp.sqrt(var + 1e-06)
    modulated = (normed * (1.0 + scale) + shift).astype(jnp.bfloat16)
    projected = jnp.dot(modulated, qkv_weight, preferred_element_type=jnp.float32)
    q_raw = projected[:, :inner].reshape(-1, HEADS, HD)
    k_raw = projected[:, inner:2 * inner].reshape(-1, HEADS, HD)
    query = (q_raw * lax.rsqrt(lax.optimization_barrier(jnp.mean(q_raw * q_raw, axis=-1, keepdims=True)) + 1e-06) * q_gain).astype(jnp.bfloat16)
    key = (k_raw * lax.rsqrt(lax.optimization_barrier(jnp.mean(k_raw * k_raw, axis=-1, keepdims=True)) + 1e-06) * k_gain).astype(jnp.bfloat16)
    value = projected[:, 2 * inner:].astype(jnp.bfloat16)
    query = query.reshape(FRAMES, HEIGHT, WIDTH, HEADS, HD)
    key = key.reshape(FRAMES, HEIGHT, WIDTH, HEADS, HD)
    value = value.reshape(FRAMES, HEIGHT, WIDTH, HEADS, HD)
    pads = ((0, 0), (TILE_H, TILE_H), (TILE_W, TILE_W), (0, 0), (0, 0))
    key_pad = jnp.pad(key, pads)
    value_pad = jnp.pad(value, pads)
    rows_ok = (jnp.arange(HEIGHT + 2 * TILE_H) >= TILE_H) & (jnp.arange(HEIGHT + 2 * TILE_H) < HEIGHT + TILE_H)
    cols_ok = (jnp.arange(WIDTH + 2 * TILE_W) >= TILE_W) & (jnp.arange(WIDTH + 2 * TILE_W) < WIDTH + TILE_W)
    valid_pad = rows_ok[:, None] & cols_ok[None, :]
    tiles_w = WIDTH // TILE_W
    tiles_h = HEIGHT // TILE_H
    groups = FRAMES // TILE_T
    zero = jnp.zeros((), jnp.int32)

    def one_tile(index):
        row0 = (index // tiles_w * TILE_H).astype(jnp.int32)
        col0 = (index % tiles_w * TILE_W).astype(jnp.int32)
        qt = lax.dynamic_slice(query, (zero, row0, col0, zero, zero), (FRAMES, TILE_H, TILE_W, HEADS, HD))
        kt = lax.dynamic_slice(key_pad, (zero, row0, col0, zero, zero), (FRAMES, 3 * TILE_H, 3 * TILE_W, HEADS, HD))
        vt = lax.dynamic_slice(value_pad, (zero, row0, col0, zero, zero), (FRAMES, 3 * TILE_H, 3 * TILE_W, HEADS, HD))
        valid = lax.dynamic_slice(valid_pad, (row0, col0), (3 * TILE_H, 3 * TILE_W))
        valid = jnp.broadcast_to(valid, (TILE_T, 3 * TILE_H, 3 * TILE_W)).reshape(-1)
        qt = qt.reshape(groups, -1, HEADS, HD).astype(jnp.float32)
        kt = kt.reshape(groups, -1, HEADS, HD).astype(jnp.float32)
        vt = vt.reshape(groups, -1, HEADS, HD).astype(jnp.float32)
        scores = jnp.einsum('bqhd,bkhd->bhqk', qt, kt) / jnp.sqrt(jnp.float32(HD))
        scores = jnp.where(valid[None, None, None, :], scores, -jnp.inf)
        top = lax.optimization_barrier(jnp.max(scores, axis=-1, keepdims=True))
        expo = jnp.exp(scores - top)
        total = lax.optimization_barrier(jnp.sum(expo, axis=-1))
        probability_rows = expo.astype(jnp.bfloat16).astype(jnp.float32)
        summed_output = jnp.einsum('bhqk,bkhd->bqhd', probability_rows, vt)
        attended = summed_output / jnp.transpose(total, (0, 2, 1))[..., None]
        return attended.reshape(FRAMES, TILE_H, TILE_W, inner).astype(jnp.bfloat16)
    tiles = lax.map(one_tile, jnp.arange(tiles_h * tiles_w, dtype=jnp.int32))
    tiles = tiles.reshape(tiles_h, tiles_w, FRAMES, TILE_H, TILE_W, inner)
    attended = jnp.transpose(tiles, (2, 0, 3, 1, 4, 5)).reshape(-1, inner)
    output = jnp.dot(attended, out_weight, preferred_element_type=jnp.float32)
    return (gate * output).astype(jnp.bfloat16).reshape(FRAMES, HEIGHT, WIDTH, D)
```

```python
import jax
import jax.numpy as jnp
from jax import lax
from jax.experimental import pallas as pl
from jax.experimental.pallas import tpu as pltpu
from jax.sharding import PartitionSpec as P

HEADS = 12
HD = 128
TILE_T = 4


def padded(x, sides, width):
    for axis, dim in sides:
        peers, length = (lax.axis_size(axis), x.shape[dim])
        up = [(i, (i + 1) % peers) for i in range(peers - 1)]
        down = [(j, i) for i, j in up]
        last = lax.slice_in_dim(x, length - width, length, axis=dim)
        initial = lax.slice_in_dim(x, 0, width, axis=dim)
        before = lax.ppermute(last, axis, up)
        after = lax.ppermute(initial, axis, down)
        x = jnp.concatenate([before, x, after], axis=dim)
    return x


def add_rows(left, piece):
    return jnp.dot(left, piece, preferred_element_type=jnp.float32)


def per_head_norm(raw, gain):
    return (raw * lax.rsqrt(jnp.mean(raw * raw, axis=-1, keepdims=True) + 1e-06) * gain).astype(
        jnp.bfloat16
    )


def shards_general(tokens, shift, scale, gate, qkv_weight, out_weight, q_gain, k_gain):
    frame_list, tile_h, tile_w, width = tokens.shape
    count = frame_list * tile_h * tile_w
    inner = HEADS * HD
    groups = frame_list // TILE_T
    tall = lax.axis_size("ha")
    wide = lax.axis_size("wa")
    flat = tokens.reshape(count, width).astype(jnp.float32)
    mean = jnp.mean(flat, axis=-1, keepdims=True)
    centred = flat - mean
    var = jnp.mean(centred * centred, axis=-1, keepdims=True)
    normed = centred / jnp.sqrt(var + 1e-06)
    modulated = (normed * (1.0 + scale) + shift).astype(jnp.bfloat16)
    projected = add_rows(modulated, lax.all_gather(qkv_weight, "wa", axis=0, tiled=True))
    query = per_head_norm(projected[:, :inner].reshape(count, HEADS, HD), q_gain)
    key = per_head_norm(projected[:, inner : 2 * inner].reshape(count, HEADS, HD), k_gain)
    value = projected[:, 2 * inner :].astype(jnp.bfloat16)
    both = jnp.concatenate(
        [
            key.reshape(frame_list, tile_h, tile_w, inner),
            value.reshape(frame_list, tile_h, tile_w, inner),
        ],
        axis=-1,
    )
    window = padded(both, (("ha", 1), ("wa", 2)), tile_h)
    rows = lax.axis_index("ha") * tile_h - tile_h + jnp.arange(3 * tile_h, dtype=jnp.int32)
    cols = lax.axis_index("wa") * tile_w - tile_w + jnp.arange(3 * tile_w, dtype=jnp.int32)
    rows_ok = (rows >= 0) & (rows < tile_h * tall)
    cols_ok = (cols >= 0) & (cols < tile_w * wide)
    valid = jnp.broadcast_to(
        rows_ok[:, None] & cols_ok[None, :], (TILE_T, 3 * tile_h, 3 * tile_w)
    ).reshape(-1)
    window = window.reshape(groups, -1, 2 * inner)
    keys = window[:, :, :inner].reshape(groups, -1, HEADS, HD)
    values = window[:, :, inner:].reshape(groups, -1, HEADS, HD)
    queries = query.reshape(groups, -1, HEADS, HD)
    inv_root = 1.0 / jnp.sqrt(jnp.float32(HD))

    def one_head(head):
        query_head_rows = lax.dynamic_index_in_dim(queries, head, 2, keepdims=False)
        key_head_rows = lax.dynamic_index_in_dim(keys, head, 2, keepdims=False)
        value_head_rows = lax.dynamic_index_in_dim(values, head, 2, keepdims=False)
        scores = (
            jnp.einsum(
                "nur,ncr->nuc", query_head_rows, key_head_rows, preferred_element_type=jnp.float32
            )
            * inv_root
        )
        scores = jnp.where(valid[None, None, :], scores, -jnp.inf)
        top = jnp.max(scores, axis=-1, keepdims=True)
        expo = jnp.exp(scores - top)
        total = jnp.sum(expo, axis=-1, keepdims=True)
        probability_rows = expo.astype(jnp.bfloat16)
        summed_output = jnp.einsum(
            "ypi,yif->ypf", probability_rows, value_head_rows, preferred_element_type=jnp.float32
        )
        return summed_output / total

    per_head = lax.map(one_head, jnp.arange(HEADS, dtype=jnp.int32))
    attended = jnp.transpose(per_head, (1, 2, 0, 3)).reshape(count, inner).astype(jnp.bfloat16)
    output = add_rows(attended, lax.all_gather(out_weight, "wa", axis=0, tiled=True))
    return (gate * output).astype(jnp.bfloat16).reshape(frame_list, tile_h, tile_w, width)


def modulate(tokens, shift, scale):
    flat = tokens.reshape(-1, tokens.shape[-1]).astype(jnp.float32)
    mean = jnp.mean(flat, axis=-1, keepdims=True)
    centred = flat - mean
    var = jnp.mean(centred * centred, axis=-1, keepdims=True)
    normed = centred / jnp.sqrt(var + 1e-06)
    return (normed * (1.0 + scale) + shift).astype(jnp.bfloat16)


def softmax_step(state, query, keys, values):
    factor = 1.4426950408889634 * HD**-0.5
    scores = lax.dot_general(
        query, keys, (((1,), (1,)), ((), ())), preferred_element_type=jnp.float32
    )
    top = jnp.max(scores, axis=-1, keepdims=True) * factor
    if state is not None:
        top = jnp.maximum(top, state[0])
    expo = jnp.exp2(scores * factor - top)
    total = jnp.sum(expo, axis=-1, keepdims=True)
    summed = jnp.dot(expo.astype(jnp.bfloat16), values, preferred_element_type=jnp.float32)
    if state is not None:
        keep = jnp.exp2(state[0] - top)
        total = total + keep * state[1]
        summed = summed + keep * state[2]
    return top, total, summed


def attend_kernel(tall, wide, each, query, left, own, right, out, tops, totals, sums):
    w = lax.axis_index("wa")
    count = query.shape[0] // tall
    mine = each * HD

    def one_head(i, carry):
        column = pl.multiple_of(i * HD, HD)
        for t in range(tall):
            low, high = max(t - 1, 0), min(t + 2, tall)
            rows = pl.ds(low * count, (high - low) * count)
            heads = query[pl.ds(t * count, count), pl.ds(column, HD)]

            def step(ref, state):
                return softmax_step(
                    state, heads, ref[rows, pl.ds(column, HD)], ref[rows, pl.ds(mine + column, HD)]
                )

            def side(ref):
                top, total, summed = step(ref, (tops[:, :1], totals[:, :1], sums[...]))
                put(top, total, summed)

            def put(top, total, summed):
                tops[...] = jnp.broadcast_to(top, tops.shape)
                totals[...] = jnp.broadcast_to(total, totals.shape)
                sums[...] = summed

            put(*step(own, None))
            pl.when(w > 0)(lambda: side(left))
            pl.when(w < wide - 1)(lambda: side(right))
            out[pl.ds(t * count, count), pl.ds(column, HD)] = (sums[...] / totals[...]).astype(
                jnp.bfloat16
            )
        return carry

    lax.fori_loop(0, each, one_head, 0)


def shards_heads(tokens, shift, scale, gate, qkv_weight, out_weight, q_gain, k_gain):
    tall, wide = lax.axis_size("ha"), lax.axis_size("wa")
    each = HEADS // tall
    inner, mine = HEADS * HD, HEADS // tall * HD
    h = lax.axis_index("ha")
    pieces = [
        lax.dynamic_slice_in_dim(qkv_weight, i * inner + h * mine, mine, axis=1) for i in range(3)
    ]
    weight = lax.all_gather(jnp.concatenate(pieces, axis=1), "wa", axis=0, tiled=True)
    modulated = lax.all_gather(modulate(tokens, shift, scale), "ha", axis=0, tiled=True)
    total = modulated.shape[0]
    projected = add_rows(modulated, weight)
    query = per_head_norm(projected[:, :mine].reshape(total, each, HD), q_gain).reshape(total, mine)
    key = per_head_norm(projected[:, mine : 2 * mine].reshape(total, each, HD), k_gain)
    value = projected[:, 2 * mine :].astype(jnp.bfloat16)
    own = jnp.concatenate([key.reshape(total, mine), value], axis=1)
    up = [(i, i + 1) for i in range(wide - 1)]
    left = lax.ppermute(own, "wa", up)
    right = lax.ppermute(own, "wa", [(j, i) for i, j in up])
    count = total // tall
    attended = pl.pallas_call(
        lambda *refs: attend_kernel(tall, wide, each, *refs),
        out_shape=jax.ShapeDtypeStruct((total, mine), jnp.bfloat16),
        in_specs=[pl.BlockSpec(memory_space=pltpu.VMEM)] * 4,
        out_specs=pl.BlockSpec(memory_space=pltpu.VMEM),
        scratch_shapes=[pltpu.VMEM((count, HD), jnp.float32)] * 3,
        compiler_params=pltpu.CompilerParams(vmem_limit_bytes=48 * 2**20),
        name="attend",
    )(query, left, own, right)
    attended = lax.all_to_all(
        attended.reshape(tall, count, mine), "ha", split_axis=0, concat_axis=0, tiled=True
    )
    attended = jnp.transpose(attended, (1, 0, 2)).reshape(count, inner)
    output = add_rows(attended, lax.all_gather(out_weight, "wa", axis=0, tiled=True))
    return (gate * output).astype(jnp.bfloat16).reshape(tokens.shape)


def shards(tokens, *rest):
    plain = HEADS % lax.axis_size("ha") or tokens.shape[0] != TILE_T
    return (shards_general if plain else shards_heads)(tokens, *rest)


def solution(mesh):
    return jax.shard_map(
        shards,
        mesh=mesh,
        in_specs=(P(None, "ha", "wa", None), P(), P(), P(), P("wa", None), P("wa", None), P(), P()),
        out_specs=P(None, "ha", "wa", None),
        check_vma=False,
    )
```

```python
import jax
import jax.numpy as jnp
from jax import lax
from jax.experimental import pallas as pl
from jax.experimental.pallas import tpu as pltpu
from jax.sharding import PartitionSpec as P

HEADS = 12
HD = 128
TILE_T = 4


def padded(x, sides, width):
    for axis, dim in sides:
        peers, length = (lax.axis_size(axis), x.shape[dim])
        up = [(i, (i + 1) % peers) for i in range(peers - 1)]
        down = [(j, i) for i, j in up]
        last = lax.slice_in_dim(x, length - width, length, axis=dim)
        initial = lax.slice_in_dim(x, 0, width, axis=dim)
        before = lax.ppermute(last, axis, up)
        after = lax.ppermute(initial, axis, down)
        x = jnp.concatenate([before, x, after], axis=dim)
    return x


def add_rows(left, piece):
    return jnp.dot(left, piece, preferred_element_type=jnp.float32)


def per_head_norm(raw, gain):
    return (raw * lax.rsqrt(jnp.mean(raw * raw, axis=-1, keepdims=True) + 1e-06) * gain).astype(
        jnp.bfloat16
    )


def shards_general(tokens, shift, scale, gate, qkv_weight, out_weight, q_gain, k_gain):
    frame_list, tile_h, tile_w, width = tokens.shape
    count = frame_list * tile_h * tile_w
    inner = HEADS * HD
    groups = frame_list // TILE_T
    tall = lax.axis_size("ha")
    wide = lax.axis_size("wa")
    flat = tokens.reshape(count, width).astype(jnp.float32)
    mean = jnp.mean(flat, axis=-1, keepdims=True)
    centred = flat - mean
    var = jnp.mean(centred * centred, axis=-1, keepdims=True)
    normed = centred / jnp.sqrt(var + 1e-06)
    modulated = (normed * (1.0 + scale) + shift).astype(jnp.bfloat16)
    projected = add_rows(modulated, lax.all_gather(qkv_weight, "wa", axis=0, tiled=True))
    query = per_head_norm(projected[:, :inner].reshape(count, HEADS, HD), q_gain)
    key = per_head_norm(projected[:, inner : 2 * inner].reshape(count, HEADS, HD), k_gain)
    value = projected[:, 2 * inner :].astype(jnp.bfloat16)
    both = jnp.concatenate(
        [
            key.reshape(frame_list, tile_h, tile_w, inner),
            value.reshape(frame_list, tile_h, tile_w, inner),
        ],
        axis=-1,
    )
    window = padded(both, (("ha", 1), ("wa", 2)), tile_h)
    rows = lax.axis_index("ha") * tile_h - tile_h + jnp.arange(3 * tile_h, dtype=jnp.int32)
    cols = lax.axis_index("wa") * tile_w - tile_w + jnp.arange(3 * tile_w, dtype=jnp.int32)
    rows_ok = (rows >= 0) & (rows < tile_h * tall)
    cols_ok = (cols >= 0) & (cols < tile_w * wide)
    valid = jnp.broadcast_to(
        rows_ok[:, None] & cols_ok[None, :], (TILE_T, 3 * tile_h, 3 * tile_w)
    ).reshape(-1)
    window = window.reshape(groups, -1, 2 * inner)
    keys = window[:, :, :inner].reshape(groups, -1, HEADS, HD)
    values = window[:, :, inner:].reshape(groups, -1, HEADS, HD)
    queries = query.reshape(groups, -1, HEADS, HD)
    inv_root = 1.0 / jnp.sqrt(jnp.float32(HD))

    def one_head(head):
        query_head_rows = lax.dynamic_index_in_dim(queries, head, 2, keepdims=False)
        key_head_rows = lax.dynamic_index_in_dim(keys, head, 2, keepdims=False)
        value_head_rows = lax.dynamic_index_in_dim(values, head, 2, keepdims=False)
        scores = (
            jnp.einsum(
                "nur,ncr->nuc", query_head_rows, key_head_rows, preferred_element_type=jnp.float32
            )
            * inv_root
        )
        scores = jnp.where(valid[None, None, :], scores, -jnp.inf)
        top = jnp.max(scores, axis=-1, keepdims=True)
        expo = jnp.exp(scores - top)
        total = jnp.sum(expo, axis=-1, keepdims=True)
        probability_rows = expo.astype(jnp.bfloat16)
        summed_output = jnp.einsum(
            "ypi,yif->ypf", probability_rows, value_head_rows, preferred_element_type=jnp.float32
        )
        return summed_output / total

    per_head = lax.map(one_head, jnp.arange(HEADS, dtype=jnp.int32))
    attended = jnp.transpose(per_head, (1, 2, 0, 3)).reshape(count, inner).astype(jnp.bfloat16)
    output = add_rows(attended, lax.all_gather(out_weight, "wa", axis=0, tiled=True))
    return (gate * output).astype(jnp.bfloat16).reshape(frame_list, tile_h, tile_w, width)


def modulate(flat, shift, scale):
    mean = jnp.mean(flat, axis=-1, keepdims=True)
    centred = flat - mean
    var = jnp.mean(centred * centred, axis=-1, keepdims=True)
    normed = centred / jnp.sqrt(var + 1e-06)
    return (normed * (1.0 + scale) + shift).astype(jnp.bfloat16)


def softmax_step(state, query, keys, values):
    factor = 1.4426950408889634 * HD**-0.5
    scores = lax.dot_general(
        query, keys, (((1,), (1,)), ((), ())), preferred_element_type=jnp.float32
    )
    top = jnp.max(scores, axis=-1, keepdims=True) * factor
    if state is not None:
        top = jnp.maximum(top, state[0])
    expo = jnp.exp2(scores * factor - top)
    total = jnp.sum(expo, axis=-1, keepdims=True)
    summed = jnp.dot(expo.astype(jnp.bfloat16), values, preferred_element_type=jnp.float32)
    if state is not None:
        keep = jnp.exp2(state[0] - top)
        total = total + keep * state[1]
        summed = summed + keep * state[2]
    return top, total, summed


MESH = pl.DeviceIdType.MESH


def block_kernel(
    wide, tokens, shift, scale, gate, qkv_weight, out_weight, q_gain, k_gain, update,
    mod, wbuf, obuf, query, kv, attended, gathered, tops, totals, sums,
    load_sem, w_send, w_recv, t_send, t_recv, f_send, kv_send, kv_recv,
    o_send, o_recv, os_send, os_recv, a_send, a_recv,
):
    h, w = lax.axis_index("ha"), lax.axis_index("wa")
    z, c = lax.div(w, 2), lax.rem(w, 2)
    x, y = lax.rem(h, 2), lax.div(h, 2)
    deep = wide // 2
    count, width = tokens.shape
    half = count // 2
    depth = qkv_weight.shape[0]
    mine = wbuf.shape[-1]
    each = mine // HD
    inner = HEADS * HD
    has_left, has_right = z > 0, z < deep - 1
    ahead, behind, sibling = (h, w + 2), (h, w - 2), (h, w + 1 - 2 * c)
    peers = [h, 2 * y + 1 - x, 2 * (1 - y) + x, 3 - h]
    far = (h, w - 1 + 2 * c)
    has_far = jnp.where(c == 0, z, deep - 1 - z) > 0
    pending = []

    def remote(src, dst, send, recv, device):
        return pltpu.make_async_remote_copy(
            src_ref=src, dst_ref=dst, send_sem=send, recv_sem=recv,
            device_id=device, device_id_type=MESH,
        )

    def send(copy, cond=None):
        if cond is None:
            copy.start()
        else:
            pl.when(cond)(copy.start)
        pending.append((copy, cond))

    def slot(kind, source):
        rows = pl.ds(pl.multiple_of(source * depth, 16), depth)
        return obuf.at[h, rows] if kind == 3 else wbuf.at[kind, rows]

    def load(kind):
        if kind == 3:
            source = out_weight.at[:, pl.ds(pl.multiple_of(h * mine, HD), mine)]
        else:
            part = (inner, 2 * inner, 0)[kind]
            source = qkv_weight.at[:, pl.ds(pl.multiple_of(part + h * mine, HD), mine)]
        return pltpu.make_async_copy(source, slot(kind, w), load_sem.at[kind])

    def pass_on(kind, step, way, device, source):
        block = slot(kind, source)
        return remote(
            block, block, w_send.at[kind, step, way], w_recv.at[kind, source], device
        )

    def send_own(kind):
        load(kind).wait()
        send(pass_on(kind, 0, 0, ahead, w), has_right)
        send(pass_on(kind, 0, 1, behind, w), has_left)
        send(pass_on(kind, 0, 2, sibling, w))

    def forward(kind, d):
        from_left, from_right = z >= d, z < deep - d
        source = w - 2 * d
        pl.when(from_left)(pass_on(kind, 2 * d - 1, 2, sibling, source).wait_recv)
        send(pass_on(kind, 2 * d - 1, 0, ahead, source), from_left & has_right)
        send(pass_on(kind, 2 * d - 1, 2, sibling, source), from_left)
        source = w + 2 * d
        pl.when(from_right)(pass_on(kind, 2 * d, 2, sibling, source).wait_recv)
        send(pass_on(kind, 2 * d, 1, behind, source), from_right & has_left)
        send(pass_on(kind, 2 * d, 2, sibling, source), from_right)

    def whole(kind):
        for i in range(deep):
            pass_on(kind, 0, 2, sibling, 2 * i + 1 - c).wait_recv()

    for kind in range(4):
        load(kind).start()

    barrier = pltpu.get_barrier_semaphore()

    def greet(device):
        pl.semaphore_signal(barrier, inc=1, device_id=device, device_id_type=MESH)

    for peer in peers[1:]:
        greet((peer, w))
    greet(sibling)
    pl.when(has_right)(lambda: greet(ahead))
    pl.when(has_left)(lambda: greet(behind))
    pl.when(has_far)(lambda: greet(far))
    more = [cond.astype(jnp.int32) for cond in (has_right, has_left, has_far)]
    pl.semaphore_wait(barrier, 4 + more[0] + more[1] + more[2])

    send_own(0)

    def norm_rows(i, carry):
        rows = pl.ds(pl.multiple_of(i * 32, 32), 32)
        mod[h, rows, :] = modulate(tokens[rows, :].astype(jnp.float32), shift[...], scale[...])
        return carry

    def piece(tile, part):
        return mod.at[tile, pl.ds(part * half, half)]

    def token_copy(peer, tile, part):
        return remote(
            piece(tile, part), piece(tile, part), t_send.at[peer, part], t_recv.at[peer, part],
            (peers[peer], w),
        )

    def token_forward(peer, part):
        tile = peers[3 - peer]
        return remote(
            piece(tile, part), piece(tile, part), f_send.at[part], t_recv.at[3, part],
            (peers[peer], w),
        )

    lax.fori_loop(0, half // 32, norm_rows, 0)
    send(token_copy(1, h, 0))
    lax.fori_loop(half // 32, count // 32, norm_rows, 0)
    send(token_copy(2, h, 1))
    send(token_copy(1, h, 1))
    send(token_copy(2, h, 0))
    send_own(1)
    forward(0, 1)
    send_own(2)
    for d in range(2, deep):
        forward(0, d)
    token_copy(1, peers[1], 0).wait_recv()
    send(token_forward(2, 0))
    token_copy(2, peers[2], 1).wait_recv()
    send(token_forward(1, 1))
    for d in range(1, deep):
        forward(1, d)
    send_own(3)
    whole(0)
    whole(1)

    def heads_norm(raw, gain):
        parts = [per_head_norm(raw[:, i * HD : (i + 1) * HD], gain) for i in range(each)]
        return jnp.concatenate(parts, axis=1)

    def halo(j, side):
        tile = peers[j]
        rows = pl.ds(pl.multiple_of(tile * count, 16), count)
        left = jnp.where(c == 0, side, 1 - side)
        return remote(
            kv.at[1, :, rows], kv.at[2 * left, :, rows], kv_send.at[side, j], kv_recv.at[side, j],
            far if side else sibling,
        )

    def keys_of(j):
        tile = peers[j]
        rows = pl.ds(pl.multiple_of(tile * count, 16), count)
        left = mod[tile]
        kv[1, 0, rows, :] = heads_norm(add_rows(left, wbuf[0]), k_gain[...])
        kv[1, 1, rows, :] = add_rows(left, wbuf[1]).astype(jnp.bfloat16)
        send(halo(j, 1), has_far)
        send(halo(j, 0))

    keys_of(0)
    forward(2, 1)
    token_copy(1, peers[1], 1).wait_recv()
    keys_of(1)
    if deep > 2:
        forward(2, 2)
    token_copy(2, peers[2], 0).wait_recv()
    keys_of(2)
    for d in range(3, deep):
        forward(2, d)
    token_forward(1, 0).wait_recv()
    token_forward(1, 1).wait_recv()
    keys_of(3)
    whole(2)
    for t in range(len(peers)):
        rows = pl.ds(t * count, count)
        query[rows, :] = heads_norm(add_rows(mod[t], wbuf[2]), q_gain[...])
    tiles = len(peers)

    def attend(place, t, first):
        low, high = max(t - 1, 0), min(t + 2, tiles)
        rows = pl.ds(low * count, (high - low) * count)

        def one_head(i, carry):
            columns = pl.ds(pl.multiple_of(i * HD, HD), HD)
            state = None
            if not first:
                state = (tops[i, t, :, :1], totals[i, t, :, :1], sums[i, t])
            top, total, summed = softmax_step(
                state,
                query[pl.ds(t * count, count), columns],
                kv[place, 0, rows, columns],
                kv[place, 1, rows, columns],
            )
            tops[i, t] = jnp.broadcast_to(top, (count, HD))
            totals[i, t] = jnp.broadcast_to(total, (count, HD))
            sums[i, t] = summed
            return carry

        lax.fori_loop(0, each, one_head, 0)

    def out_copy(j, tile, part):
        rows = pl.ds(pl.multiple_of(part * (inner // 2), 16), inner // 2)
        return obuf.at[tile, rows]

    def out_share(j):
        block = out_copy(j, h, c)
        return remote(block, block, o_send.at[j], o_recv.at[j], (peers[j], w))

    def out_sibling(j, part):
        block = out_copy(j, peers[j], part)
        return remote(block, block, os_send.at[j], os_recv.at[j], sibling)

    for t in range(tiles):
        attend(1, t, True)
        if 1 <= t < deep:
            forward(3, t)
    for d in range(tiles, deep):
        forward(3, d)
    whole(3)
    for j in range(1, tiles):
        send(out_share(j))
    for j in range(tiles):
        halo(j, 0).wait_recv()
    for t in range(tiles):
        attend(2 - 2 * c, t, False)
    for j in range(tiles):
        pl.when(has_far)(halo(j, 1).wait_recv)

    def attended_copy(tile, source, slot):
        rows = pl.ds(pl.multiple_of(tile * count, 16), count)
        columns = pl.ds(pl.multiple_of(source * mine, HD), mine)
        return remote(
            attended.at[rows], gathered.at[:, columns], a_send.at[slot], a_recv.at[source], (tile, w)
        )

    for t in range(tiles):
        pl.when(has_far)(lambda: attend(2 * c, t, False))
        parts = [(sums[i, t] / totals[i, t]).astype(jnp.bfloat16) for i in range(each)]
        block = jnp.concatenate(parts, axis=1)
        attended[pl.ds(t * count, count), :] = block
        send(attended_copy(t, h, t), h != t)

        def keep():
            gathered[:, pl.ds(pl.multiple_of(h * mine, HD), mine)] = block

        pl.when(h == t)(keep)

    for j in range(1, tiles):
        out_copy_in = remote(
            out_copy(j, peers[j], c), out_copy(j, peers[j], c), o_send.at[j], o_recv.at[j],
            (peers[j], w),
        )
        out_copy_in.wait_recv()
        send(out_sibling(j, c))
    for s in range(tiles):
        pl.when(h != s)(attended_copy(h, s, s).wait_recv)
    for j in range(1, tiles):
        out_sibling(j, 1 - c).wait_recv()
    for q in range(tiles):
        columns = slice(q * mine, (q + 1) * mine)
        update[:, columns] = (gate[:, columns] * add_rows(gathered[...], obuf[q])).astype(
            jnp.bfloat16
        )
    for copy, cond in pending:
        if cond is None:
            copy.wait_send()
        else:
            pl.when(cond)(copy.wait_send)


def shards_heads(tokens, shift, scale, gate, qkv_weight, out_weight, q_gain, k_gain):
    tall, wide = lax.axis_size("ha"), lax.axis_size("wa")
    each = HEADS // tall
    inner, mine = HEADS * HD, HEADS // tall * HD
    width = tokens.shape[-1]
    flat = tokens.reshape(-1, width)
    count = flat.shape[0]
    vmem = pl.BlockSpec(memory_space=pltpu.VMEM)
    hbm = pl.BlockSpec(memory_space=pl.ANY)
    dma = pltpu.SemaphoreType.DMA
    state = pltpu.VMEM((each, tall, count, HD), jnp.float32)
    update = pl.pallas_call(
        lambda *refs: block_kernel(wide, *refs),
        out_shape=jax.ShapeDtypeStruct((count, width), jnp.bfloat16),
        in_specs=[vmem, vmem, vmem, vmem, hbm, hbm, vmem, vmem],
        out_specs=vmem,
        scratch_shapes=[
            pltpu.VMEM((tall, count, width), jnp.bfloat16),
            pltpu.VMEM((3, width, mine), jnp.bfloat16),
            pltpu.VMEM((tall, inner, mine), jnp.bfloat16),
            pltpu.VMEM((tall * count, mine), jnp.bfloat16),
            pltpu.VMEM((3, 2, tall * count, mine), jnp.bfloat16),
            pltpu.VMEM((tall * count, mine), jnp.bfloat16),
            pltpu.VMEM((count, inner), jnp.bfloat16),
            state,
            state,
            state,
            dma((4,)),
            dma((4, wide, 3)),
            dma((4, wide)),
            dma((3, 2)),
            dma((4, 2)),
            dma((2,)),
            dma((2, tall)),
            dma((2, tall)),
            dma((tall,)),
            dma((tall,)),
            dma((tall,)),
            dma((tall,)),
            dma((tall,)),
            dma((tall,)),
        ],
        compiler_params=pltpu.CompilerParams(
            collective_id=0, has_side_effects=True, vmem_limit_bytes=56 * 2**20
        ),
        cost_estimate=pl.CostEstimate(
            flops=9 * 10**9, bytes_accessed=4 * 10**6, transcendentals=6 * 10**6
        ),
        name="block",
    )(flat, shift[None], scale[None], gate[None], qkv_weight, out_weight, q_gain[None], k_gain[None])
    return update.reshape(tokens.shape)


def shards(tokens, *rest):
    plain = lax.axis_size("ha") != 4 or lax.axis_size("wa") % 2 or tokens.shape[0] != TILE_T
    return (shards_general if plain else shards_heads)(tokens, *rest)


def solution(mesh):
    return jax.shard_map(
        shards,
        mesh=mesh,
        in_specs=(P(None, "ha", "wa", None), P(), P(), P(), P("wa", None), P("wa", None), P(), P()),
        out_specs=P(None, "ha", "wa", None),
        check_vma=False,
    )
```

```python
import jax
import jax.numpy as jnp
from jax import lax
from jax.experimental import pallas as pl
from jax.experimental.pallas import tpu as pltpu
from jax.sharding import PartitionSpec as P

HEADS = 12
HD = 128
TILE_T = 4


def padded(x, sides, width):
    for axis, dim in sides:
        peers, length = (lax.axis_size(axis), x.shape[dim])
        up = [(i, (i + 1) % peers) for i in range(peers - 1)]
        down = [(j, i) for i, j in up]
        last = lax.slice_in_dim(x, length - width, length, axis=dim)
        initial = lax.slice_in_dim(x, 0, width, axis=dim)
        before = lax.ppermute(last, axis, up)
        after = lax.ppermute(initial, axis, down)
        x = jnp.concatenate([before, x, after], axis=dim)
    return x


def add_rows(left, piece):
    return jnp.dot(left, piece, preferred_element_type=jnp.float32)


def per_head_norm(raw, gain):
    return (raw * lax.rsqrt(jnp.mean(raw * raw, axis=-1, keepdims=True) + 1e-06) * gain).astype(
        jnp.bfloat16
    )


def shards_general(tokens, shift, scale, gate, qkv_weight, out_weight, q_gain, k_gain):
    frame_list, tile_h, tile_w, width = tokens.shape
    count = frame_list * tile_h * tile_w
    inner = HEADS * HD
    groups = frame_list // TILE_T
    tall = lax.axis_size("ha")
    wide = lax.axis_size("wa")
    flat = tokens.reshape(count, width).astype(jnp.float32)
    mean = jnp.mean(flat, axis=-1, keepdims=True)
    centred = flat - mean
    var = jnp.mean(centred * centred, axis=-1, keepdims=True)
    normed = centred / jnp.sqrt(var + 1e-06)
    modulated = (normed * (1.0 + scale) + shift).astype(jnp.bfloat16)
    projected = add_rows(modulated, lax.all_gather(qkv_weight, "wa", axis=0, tiled=True))
    query = per_head_norm(projected[:, :inner].reshape(count, HEADS, HD), q_gain)
    key = per_head_norm(projected[:, inner : 2 * inner].reshape(count, HEADS, HD), k_gain)
    value = projected[:, 2 * inner :].astype(jnp.bfloat16)
    both = jnp.concatenate(
        [
            key.reshape(frame_list, tile_h, tile_w, inner),
            value.reshape(frame_list, tile_h, tile_w, inner),
        ],
        axis=-1,
    )
    window = padded(both, (("ha", 1), ("wa", 2)), tile_h)
    rows = lax.axis_index("ha") * tile_h - tile_h + jnp.arange(3 * tile_h, dtype=jnp.int32)
    cols = lax.axis_index("wa") * tile_w - tile_w + jnp.arange(3 * tile_w, dtype=jnp.int32)
    rows_ok = (rows >= 0) & (rows < tile_h * tall)
    cols_ok = (cols >= 0) & (cols < tile_w * wide)
    valid = jnp.broadcast_to(
        rows_ok[:, None] & cols_ok[None, :], (TILE_T, 3 * tile_h, 3 * tile_w)
    ).reshape(-1)
    window = window.reshape(groups, -1, 2 * inner)
    keys = window[:, :, :inner].reshape(groups, -1, HEADS, HD)
    values = window[:, :, inner:].reshape(groups, -1, HEADS, HD)
    queries = query.reshape(groups, -1, HEADS, HD)
    inv_root = 1.0 / jnp.sqrt(jnp.float32(HD))

    def one_head(head):
        query_head_rows = lax.dynamic_index_in_dim(queries, head, 2, keepdims=False)
        key_head_rows = lax.dynamic_index_in_dim(keys, head, 2, keepdims=False)
        value_head_rows = lax.dynamic_index_in_dim(values, head, 2, keepdims=False)
        scores = (
            jnp.einsum(
                "nur,ncr->nuc", query_head_rows, key_head_rows, preferred_element_type=jnp.float32
            )
            * inv_root
        )
        scores = jnp.where(valid[None, None, :], scores, -jnp.inf)
        top = jnp.max(scores, axis=-1, keepdims=True)
        expo = jnp.exp(scores - top)
        total = jnp.sum(expo, axis=-1, keepdims=True)
        probability_rows = expo.astype(jnp.bfloat16)
        summed_output = jnp.einsum(
            "ypi,yif->ypf", probability_rows, value_head_rows, preferred_element_type=jnp.float32
        )
        return summed_output / total

    per_head = lax.map(one_head, jnp.arange(HEADS, dtype=jnp.int32))
    attended = jnp.transpose(per_head, (1, 2, 0, 3)).reshape(count, inner).astype(jnp.bfloat16)
    output = add_rows(attended, lax.all_gather(out_weight, "wa", axis=0, tiled=True))
    return (gate * output).astype(jnp.bfloat16).reshape(frame_list, tile_h, tile_w, width)


def modulate(flat, shift, scale):
    mean = jnp.mean(flat, axis=-1, keepdims=True)
    centred = flat - mean
    var = jnp.mean(centred * centred, axis=-1, keepdims=True)
    normed = centred / jnp.sqrt(var + 1e-06)
    return (normed * (1.0 + scale) + shift).astype(jnp.bfloat16)


def softmax_step(state, query, keys, values):
    factor = 1.4426950408889634 * HD**-0.5
    scores = lax.dot_general(
        query, keys, (((1,), (1,)), ((), ())), preferred_element_type=jnp.float32
    )
    top = jnp.max(scores, axis=-1, keepdims=True) * factor
    if state is not None:
        top = jnp.maximum(top, state[0])
    expo = jnp.exp2(scores * factor - top)
    total = jnp.sum(expo, axis=-1, keepdims=True)
    summed = jnp.dot(expo.astype(jnp.bfloat16), values, preferred_element_type=jnp.float32)
    if state is not None:
        keep = jnp.exp2(state[0] - top)
        total = total + keep * state[1]
        summed = summed + keep * state[2]
    return top, total, summed


MESH = pl.DeviceIdType.MESH


def block_kernel(
    wide, tokens, shift, scale, gate, qkv_weight, out_weight, q_gain, k_gain, update,
    mod, wbuf, obuf, query, kv, attended, gathered, tops, totals, sums,
    load_sem, w_send, w_recv, t_send, t_recv, f_send, kv_send, kv_recv,
    o_send, o_recv, of_send, of_recv, os_send, os_recv, a_send, a_recv,
):
    h, w = lax.axis_index("ha"), lax.axis_index("wa")
    z, c = lax.div(w, 2), lax.rem(w, 2)
    x, y = lax.rem(h, 2), lax.div(h, 2)
    deep = wide // 2
    count, width = tokens.shape
    half = count // 2
    depth = qkv_weight.shape[0]
    mine = wbuf.shape[-1]
    each = mine // HD
    inner = HEADS * HD
    has_left, has_right = z > 0, z < deep - 1
    ahead, behind, sibling = (h, w + 2), (h, w - 2), (h, w + 1 - 2 * c)
    peers = [h, 2 * y + 1 - x, 2 * (1 - y) + x, 3 - h]
    far = (h, w - 1 + 2 * c)
    has_far = jnp.where(c == 0, z, deep - 1 - z) > 0
    pending = []

    def remote(src, dst, send, recv, device):
        return pltpu.make_async_remote_copy(
            src_ref=src, dst_ref=dst, send_sem=send, recv_sem=recv,
            device_id=device, device_id_type=MESH,
        )

    def send(copy, cond=None):
        if cond is None:
            copy.start()
        else:
            pl.when(cond)(copy.start)
        pending.append((copy, cond))

    def slot(kind, source):
        if kind == 3:
            return obuf.at[h, lax.div(source, 2), lax.rem(source, 2)]
        return wbuf.at[kind, pl.ds(pl.multiple_of(source * depth, 16), depth)]

    def load(kind):
        if kind == 3:
            source = out_weight.at[:, pl.ds(pl.multiple_of(h * mine, HD), mine)]
        else:
            part = (inner, 2 * inner, 0)[kind]
            source = qkv_weight.at[:, pl.ds(pl.multiple_of(part + h * mine, HD), mine)]
        return pltpu.make_async_copy(source, slot(kind, w), load_sem.at[kind])

    def pass_on(kind, step, way, device, source):
        block = slot(kind, source)
        return remote(
            block, block, w_send.at[kind, step, way], w_recv.at[kind, source], device
        )

    def send_own(kind):
        load(kind).wait()
        send(pass_on(kind, 0, 0, ahead, w), has_right)
        send(pass_on(kind, 0, 1, behind, w), has_left)
        send(pass_on(kind, 0, 2, sibling, w))
        if kind == 3:
            share_out(w, None)

    def share_out(source, cond):
        block, layer = slot(3, source), lax.div(source, 2)
        for j in (1, 2):
            send(
                remote(block, block, o_send.at[j, layer], o_recv.at[j, layer], (peers[j], w)), cond
            )

    def forward(kind, d):
        from_left, from_right = z >= d, z < deep - d
        source = w - 2 * d
        pl.when(from_left)(pass_on(kind, 2 * d - 1, 2, sibling, source).wait_recv)
        send(pass_on(kind, 2 * d - 1, 0, ahead, source), from_left & has_right)
        send(pass_on(kind, 2 * d - 1, 2, sibling, source), from_left)
        if kind == 3:
            share_out(source, from_left)
        source = w + 2 * d
        pl.when(from_right)(pass_on(kind, 2 * d, 2, sibling, source).wait_recv)
        send(pass_on(kind, 2 * d, 1, behind, source), from_right & has_left)
        send(pass_on(kind, 2 * d, 2, sibling, source), from_right)
        if kind == 3:
            share_out(source, from_right)

    def whole(kind):
        for i in range(deep):
            pass_on(kind, 0, 2, sibling, 2 * i + 1 - c).wait_recv()

    for kind in range(4):
        load(kind).start()

    barrier = pltpu.get_barrier_semaphore()

    def greet(device):
        pl.semaphore_signal(barrier, inc=1, device_id=device, device_id_type=MESH)

    for peer in peers[1:]:
        greet((peer, w))
    greet(sibling)
    pl.when(has_right)(lambda: greet(ahead))
    pl.when(has_left)(lambda: greet(behind))
    pl.when(has_far)(lambda: greet(far))
    more = [cond.astype(jnp.int32) for cond in (has_right, has_left, has_far)]
    pl.semaphore_wait(barrier, 4 + more[0] + more[1] + more[2])

    send_own(0)

    def norm_rows(i, carry):
        rows = pl.ds(pl.multiple_of(i * 32, 32), 32)
        mod[h, rows, :] = modulate(tokens[rows, :].astype(jnp.float32), shift[...], scale[...])
        return carry

    def piece(tile, part):
        return mod.at[tile, pl.ds(part * half, half)]

    def token_copy(peer, tile, part):
        return remote(
            piece(tile, part), piece(tile, part), t_send.at[peer, part], t_recv.at[peer, part],
            (peers[peer], w),
        )

    def token_forward(peer, part):
        tile = peers[3 - peer]
        return remote(
            piece(tile, part), piece(tile, part), f_send.at[part], t_recv.at[3, part],
            (peers[peer], w),
        )

    lax.fori_loop(0, half // 32, norm_rows, 0)
    send(token_copy(1, h, 0))
    lax.fori_loop(half // 32, count // 32, norm_rows, 0)
    send(token_copy(2, h, 1))
    send(token_copy(1, h, 1))
    send(token_copy(2, h, 0))
    send_own(1)
    forward(0, 1)
    send_own(2)
    for d in range(2, deep):
        forward(0, d)
    token_copy(1, peers[1], 0).wait_recv()
    send(token_forward(2, 0))
    token_copy(2, peers[2], 1).wait_recv()
    send(token_forward(1, 1))
    for d in range(1, deep):
        forward(1, d)
    send_own(3)
    whole(0)
    whole(1)

    def heads_norm(raw, gain):
        parts = [per_head_norm(raw[:, i * HD : (i + 1) * HD], gain) for i in range(each)]
        return jnp.concatenate(parts, axis=1)

    def halo(j, side):
        tile = peers[j]
        rows = pl.ds(pl.multiple_of(tile * count, 16), count)
        left = jnp.where(c == 0, side, 1 - side)
        return remote(
            kv.at[1, :, rows], kv.at[2 * left, :, rows], kv_send.at[side, j], kv_recv.at[side, j],
            far if side else sibling,
        )

    def keys_of(j):
        tile = peers[j]
        rows = pl.ds(pl.multiple_of(tile * count, 16), count)
        left = mod[tile]
        kv[1, 0, rows, :] = heads_norm(add_rows(left, wbuf[0]), k_gain[...])
        kv[1, 1, rows, :] = add_rows(left, wbuf[1]).astype(jnp.bfloat16)
        send(halo(j, 1), has_far)
        send(halo(j, 0))

    keys_of(0)
    forward(2, 1)
    token_copy(1, peers[1], 1).wait_recv()
    keys_of(1)
    if deep > 2:
        forward(2, 2)
    token_copy(2, peers[2], 0).wait_recv()
    keys_of(2)
    for d in range(3, deep):
        forward(2, d)
    forward(3, 1)
    token_forward(1, 0).wait_recv()
    token_forward(1, 1).wait_recv()
    keys_of(3)
    if deep > 2:
        forward(3, 2)
    whole(2)
    for t in range(len(peers)):
        rows = pl.ds(t * count, count)
        query[rows, :] = heads_norm(add_rows(mod[t], wbuf[2]), q_gain[...])
    tiles = len(peers)

    def attend(place, t, first):
        low, high = max(t - 1, 0), min(t + 2, tiles)
        rows = pl.ds(low * count, (high - low) * count)

        for i in range(each):
            columns = pl.ds(i * HD, HD)
            state = None
            if not first:
                state = (tops[i, t, :, :1], totals[i, t, :, :1], sums[i, t])
            top, total, summed = softmax_step(
                state,
                query[pl.ds(t * count, count), columns],
                kv[place, 0, rows, columns],
                kv[place, 1, rows, columns],
            )
            tops[i, t] = jnp.broadcast_to(top, (count, HD))
            totals[i, t] = jnp.broadcast_to(total, (count, HD))
            sums[i, t] = summed

    def out_forward(peer, part):
        first, size = (0, deep // 2) if part == 0 else (deep // 2, deep - deep // 2)
        block = obuf.at[peers[3 - peer], pl.ds(first, size), c]
        return remote(block, block, of_send.at[part], of_recv.at[part], (peers[peer], w))

    def out_sibling(j, core):
        block = obuf.at[peers[j], :, core]
        return remote(block, block, os_send.at[j], os_recv.at[j], sibling)

    for d in range(3, deep):
        forward(3, d)
    for t in range(tiles):
        attend(1, t, True)
    for j in range(tiles):
        halo(j, 0).wait_recv()
    for t in range(tiles):
        attend(2 - 2 * c, t, False)
        if t == 1:
            for j in (1, 2):
                for layer in range(deep):
                    block = obuf.at[peers[j], layer, c]
                    remote(
                        block, block, o_send.at[j, layer], o_recv.at[j, layer], (peers[j], w)
                    ).wait_recv()
                send(out_forward(3 - j, j - 1))
            for j in (1, 2):
                send(out_sibling(j, c))
    for j in range(tiles):
        pl.when(has_far)(halo(j, 1).wait_recv)

    def attended_copy(tile, source, slot):
        rows = pl.ds(pl.multiple_of(tile * count, 16), count)
        columns = pl.ds(pl.multiple_of(source * mine, HD), mine)
        return remote(
            attended.at[rows], gathered.at[:, columns], a_send.at[slot], a_recv.at[source], (tile, w)
        )

    for t in range(tiles):
        pl.when(has_far)(lambda: attend(2 * c, t, False))
        parts = [(sums[i, t] / totals[i, t]).astype(jnp.bfloat16) for i in range(each)]
        block = jnp.concatenate(parts, axis=1)
        attended[pl.ds(t * count, count), :] = block
        send(attended_copy(t, h, t), h != t)

        def keep():
            gathered[:, pl.ds(pl.multiple_of(h * mine, HD), mine)] = block

        pl.when(h == t)(keep)

    for part in range(2):
        out_forward(2 - part, part).wait_recv()
    send(out_sibling(3, c))
    whole(3)
    for s in range(tiles):
        pl.when(h != s)(attended_copy(h, s, s).wait_recv)
    for j in range(1, tiles):
        out_sibling(j, 1 - c).wait_recv()
    for q in range(tiles):
        columns = slice(q * mine, (q + 1) * mine)
        product = add_rows(gathered[...], obuf[q].reshape(inner, mine))
        update[:, columns] = (gate[columns] * product).astype(jnp.bfloat16)
    for copy, cond in pending:
        if cond is None:
            copy.wait_send()
        else:
            pl.when(cond)(copy.wait_send)


def shards_heads(tokens, shift, scale, gate, qkv_weight, out_weight, q_gain, k_gain):
    tall, wide = lax.axis_size("ha"), lax.axis_size("wa")
    each = HEADS // tall
    inner, mine = HEADS * HD, HEADS // tall * HD
    width = tokens.shape[-1]
    flat = tokens.reshape(-1, width)
    count = flat.shape[0]
    vmem = pl.BlockSpec(memory_space=pltpu.VMEM)
    hbm = pl.BlockSpec(memory_space=pl.ANY)
    dma = pltpu.SemaphoreType.DMA
    state = pltpu.VMEM((each, tall, count, HD), jnp.float32)
    update = pl.pallas_call(
        lambda *refs: block_kernel(wide, *refs),
        out_shape=jax.ShapeDtypeStruct((count, width), jnp.bfloat16),
        in_specs=[vmem, vmem, vmem, vmem, hbm, hbm, vmem, vmem],
        out_specs=vmem,
        scratch_shapes=[
            pltpu.VMEM((tall, count, width), jnp.bfloat16),
            pltpu.VMEM((3, width, mine), jnp.bfloat16),
            pltpu.VMEM((tall, wide // 2, 2, inner // wide, mine), jnp.bfloat16),
            pltpu.VMEM((tall * count, mine), jnp.bfloat16),
            pltpu.VMEM((3, 2, tall * count, mine), jnp.bfloat16),
            pltpu.VMEM((tall * count, mine), jnp.bfloat16),
            pltpu.VMEM((count, inner), jnp.bfloat16),
            state,
            state,
            state,
            dma((4,)),
            dma((4, wide, 3)),
            dma((4, wide)),
            dma((3, 2)),
            dma((4, 2)),
            dma((2,)),
            dma((2, tall)),
            dma((2, tall)),
            dma((3, wide // 2)),
            dma((3, wide // 2)),
            dma((2,)),
            dma((2,)),
            dma((tall,)),
            dma((tall,)),
            dma((tall,)),
            dma((tall,)),
        ],
        compiler_params=pltpu.CompilerParams(
            collective_id=0, has_side_effects=True, vmem_limit_bytes=56 * 2**20
        ),
        cost_estimate=pl.CostEstimate(
            flops=9 * 10**9, bytes_accessed=4 * 10**6, transcendentals=6 * 10**6
        ),
        name="block",
    )(flat, shift, scale, gate, qkv_weight, out_weight, q_gain, k_gain)
    return update.reshape(tokens.shape)


def shards(tokens, *rest):
    plain = lax.axis_size("ha") != 4 or lax.axis_size("wa") % 2 or tokens.shape[0] != TILE_T
    return (shards_general if plain else shards_heads)(tokens, *rest)


def solution(mesh):
    return jax.shard_map(
        shards,
        mesh=mesh,
        in_specs=(P(None, "ha", "wa", None), P(), P(), P(), P("wa", None), P("wa", None), P(), P()),
        out_specs=P(None, "ha", "wa", None),
        check_vma=False,
    )
```

```python
import jax
import jax.numpy as jnp
from jax import lax
from jax.experimental import pallas as pl
from jax.experimental.pallas import tpu as pltpu
from jax.sharding import PartitionSpec as P

HEADS = 12
HD = 128
TILE_T = 4


def padded(x, sides, width):
    for axis, dim in sides:
        peers, length = (lax.axis_size(axis), x.shape[dim])
        up = [(i, (i + 1) % peers) for i in range(peers - 1)]
        down = [(j, i) for i, j in up]
        last = lax.slice_in_dim(x, length - width, length, axis=dim)
        initial = lax.slice_in_dim(x, 0, width, axis=dim)
        before = lax.ppermute(last, axis, up)
        after = lax.ppermute(initial, axis, down)
        x = jnp.concatenate([before, x, after], axis=dim)
    return x


def add_rows(left, piece):
    return jnp.dot(left, piece, preferred_element_type=jnp.float32)


def per_head_norm(raw, gain):
    return (raw * lax.rsqrt(jnp.mean(raw * raw, axis=-1, keepdims=True) + 1e-06) * gain).astype(
        jnp.bfloat16
    )


def shards_general(tokens, shift, scale, gate, qkv_weight, out_weight, q_gain, k_gain):
    frame_list, tile_h, tile_w, width = tokens.shape
    count = frame_list * tile_h * tile_w
    inner = HEADS * HD
    groups = frame_list // TILE_T
    tall = lax.axis_size("ha")
    wide = lax.axis_size("wa")
    flat = tokens.reshape(count, width).astype(jnp.float32)
    mean = jnp.mean(flat, axis=-1, keepdims=True)
    centred = flat - mean
    var = jnp.mean(centred * centred, axis=-1, keepdims=True)
    normed = centred / jnp.sqrt(var + 1e-06)
    modulated = (normed * (1.0 + scale) + shift).astype(jnp.bfloat16)
    projected = add_rows(modulated, lax.all_gather(qkv_weight, "wa", axis=0, tiled=True))
    query = per_head_norm(projected[:, :inner].reshape(count, HEADS, HD), q_gain)
    key = per_head_norm(projected[:, inner : 2 * inner].reshape(count, HEADS, HD), k_gain)
    value = projected[:, 2 * inner :].astype(jnp.bfloat16)
    both = jnp.concatenate(
        [
            key.reshape(frame_list, tile_h, tile_w, inner),
            value.reshape(frame_list, tile_h, tile_w, inner),
        ],
        axis=-1,
    )
    window = padded(both, (("ha", 1), ("wa", 2)), tile_h)
    rows = lax.axis_index("ha") * tile_h - tile_h + jnp.arange(3 * tile_h, dtype=jnp.int32)
    cols = lax.axis_index("wa") * tile_w - tile_w + jnp.arange(3 * tile_w, dtype=jnp.int32)
    rows_ok = (rows >= 0) & (rows < tile_h * tall)
    cols_ok = (cols >= 0) & (cols < tile_w * wide)
    valid = jnp.broadcast_to(
        rows_ok[:, None] & cols_ok[None, :], (TILE_T, 3 * tile_h, 3 * tile_w)
    ).reshape(-1)
    window = window.reshape(groups, -1, 2 * inner)
    keys = window[:, :, :inner].reshape(groups, -1, HEADS, HD)
    values = window[:, :, inner:].reshape(groups, -1, HEADS, HD)
    queries = query.reshape(groups, -1, HEADS, HD)
    inv_root = 1.0 / jnp.sqrt(jnp.float32(HD))

    def one_head(head):
        query_head_rows = lax.dynamic_index_in_dim(queries, head, 2, keepdims=False)
        key_head_rows = lax.dynamic_index_in_dim(keys, head, 2, keepdims=False)
        value_head_rows = lax.dynamic_index_in_dim(values, head, 2, keepdims=False)
        scores = (
            jnp.einsum(
                "nur,ncr->nuc", query_head_rows, key_head_rows, preferred_element_type=jnp.float32
            )
            * inv_root
        )
        scores = jnp.where(valid[None, None, :], scores, -jnp.inf)
        top = jnp.max(scores, axis=-1, keepdims=True)
        expo = jnp.exp(scores - top)
        total = jnp.sum(expo, axis=-1, keepdims=True)
        probability_rows = expo.astype(jnp.bfloat16)
        summed_output = jnp.einsum(
            "ypi,yif->ypf", probability_rows, value_head_rows, preferred_element_type=jnp.float32
        )
        return summed_output / total

    per_head = lax.map(one_head, jnp.arange(HEADS, dtype=jnp.int32))
    attended = jnp.transpose(per_head, (1, 2, 0, 3)).reshape(count, inner).astype(jnp.bfloat16)
    output = add_rows(attended, lax.all_gather(out_weight, "wa", axis=0, tiled=True))
    return (gate * output).astype(jnp.bfloat16).reshape(frame_list, tile_h, tile_w, width)


def modulate(flat, shift, scale):
    mean = jnp.mean(flat, axis=-1, keepdims=True)
    centred = flat - mean
    var = jnp.mean(centred * centred, axis=-1, keepdims=True)
    normed = centred / jnp.sqrt(var + 1e-06)
    return (normed * (1.0 + scale) + shift).astype(jnp.bfloat16)


def softmax_step(state, query, keys, values):
    factor = 1.4426950408889634 * HD**-0.5
    scores = lax.dot_general(
        query, keys, (((1,), (1,)), ((), ())), preferred_element_type=jnp.float32
    )
    top = jnp.max(scores, axis=-1, keepdims=True) * factor
    if state is not None:
        top = jnp.maximum(top, state[0])
    expo = jnp.exp2(scores * factor - top)
    total = jnp.sum(expo, axis=-1, keepdims=True)
    summed = jnp.dot(expo.astype(jnp.bfloat16), values, preferred_element_type=jnp.float32)
    if state is not None:
        keep = jnp.exp2(state[0] - top)
        total = total + keep * state[1]
        summed = summed + keep * state[2]
    return top, total, summed


MESH = pl.DeviceIdType.MESH


def block_kernel(
    wide, tokens, shift, scale, gate, qkv_weight, out_weight, q_gain, k_gain, update,
    mod, wbuf, obuf, query, kv, attended, gathered, tops, totals, sums,
    load_sem, w_send, w_recv, t_send, t_recv, f_send, kv_send, kv_recv,
    o_send, o_recv, of_send, of_recv, os_send, os_recv, a_send, a_recv,
):
    h, w = lax.axis_index("ha"), lax.axis_index("wa")
    z, c = lax.div(w, 2), lax.rem(w, 2)
    x, y = lax.rem(h, 2), lax.div(h, 2)
    deep = wide // 2
    count, width = tokens.shape
    half = count // 2
    depth = qkv_weight.shape[0]
    mine = wbuf.shape[-1]
    each = mine // HD
    inner = HEADS * HD
    has_left, has_right = z > 0, z < deep - 1
    ahead, behind, sibling = (h, w + 2), (h, w - 2), (h, w + 1 - 2 * c)
    peers = [h, 2 * y + 1 - x, 2 * (1 - y) + x, 3 - h]
    far = (h, w - 1 + 2 * c)
    has_far = jnp.where(c == 0, z, deep - 1 - z) > 0
    pending = []

    def remote(src, dst, send, recv, device):
        return pltpu.make_async_remote_copy(
            src_ref=src, dst_ref=dst, send_sem=send, recv_sem=recv,
            device_id=device, device_id_type=MESH,
        )

    def send(copy, cond=None):
        if cond is None:
            copy.start()
        else:
            pl.when(cond)(copy.start)
        pending.append((copy, cond))

    def slot(kind, source):
        if kind == 3:
            return obuf.at[h, lax.div(source, 2), lax.rem(source, 2)]
        return wbuf.at[kind, pl.ds(pl.multiple_of(source * depth, 16), depth)]

    def load(kind):
        if kind == 3:
            source = out_weight.at[:, pl.ds(pl.multiple_of(h * mine, HD), mine)]
        else:
            part = (inner, 2 * inner, 0)[kind]
            source = qkv_weight.at[:, pl.ds(pl.multiple_of(part + h * mine, HD), mine)]
        return pltpu.make_async_copy(source, slot(kind, w), load_sem.at[kind])

    def pass_on(kind, step, way, device, source):
        block = slot(kind, source)
        return remote(
            block, block, w_send.at[kind, step, way], w_recv.at[kind, source], device
        )

    def send_own(kind):
        load(kind).wait()
        send(pass_on(kind, 0, 0, ahead, w), has_right)
        send(pass_on(kind, 0, 1, behind, w), has_left)
        send(pass_on(kind, 0, 2, sibling, w))
        if kind == 3:
            share_out(w, None)

    def share_out(source, cond):
        block, layer = slot(3, source), lax.div(source, 2)
        for j in (1, 2):
            send(
                remote(block, block, o_send.at[j, layer], o_recv.at[j, layer], (peers[j], w)), cond
            )

    def forward(kind, d):
        from_left, from_right = z >= d, z < deep - d
        source = w - 2 * d
        pl.when(from_left)(pass_on(kind, 2 * d - 1, 2, sibling, source).wait_recv)
        send(pass_on(kind, 2 * d - 1, 0, ahead, source), from_left & has_right)
        send(pass_on(kind, 2 * d - 1, 2, sibling, source), from_left)
        if kind == 3:
            share_out(source, from_left)
        source = w + 2 * d
        pl.when(from_right)(pass_on(kind, 2 * d, 2, sibling, source).wait_recv)
        send(pass_on(kind, 2 * d, 1, behind, source), from_right & has_left)
        send(pass_on(kind, 2 * d, 2, sibling, source), from_right)
        if kind == 3:
            share_out(source, from_right)

    def whole(kind):
        for i in range(deep):
            pass_on(kind, 0, 2, sibling, 2 * i + 1 - c).wait_recv()

    for kind in range(4):
        load(kind).start()

    barrier = pltpu.get_barrier_semaphore()

    def greet(device):
        pl.semaphore_signal(barrier, inc=1, device_id=device, device_id_type=MESH)

    for peer in peers[1:]:
        greet((peer, w))
    greet(sibling)
    pl.when(has_right)(lambda: greet(ahead))
    pl.when(has_left)(lambda: greet(behind))
    pl.when(has_far)(lambda: greet(far))
    more = [cond.astype(jnp.int32) for cond in (has_right, has_left, has_far)]
    pl.semaphore_wait(barrier, 4 + more[0] + more[1] + more[2])

    send_own(0)

    def norm_rows(i, carry):
        rows = pl.ds(pl.multiple_of(i * 32, 32), 32)
        mod[h, rows, :] = modulate(tokens[rows, :].astype(jnp.float32), shift[...], scale[...])
        return carry

    def piece(tile, part):
        return mod.at[tile, pl.ds(part * half, half)]

    def token_copy(peer, tile, part):
        return remote(
            piece(tile, part), piece(tile, part), t_send.at[peer, part], t_recv.at[peer, part],
            (peers[peer], w),
        )

    def token_forward(peer, part):
        tile = peers[3 - peer]
        return remote(
            piece(tile, part), piece(tile, part), f_send.at[part], t_recv.at[3, part],
            (peers[peer], w),
        )

    lax.fori_loop(0, half // 32, norm_rows, 0)
    send(token_copy(1, h, 0))
    lax.fori_loop(half // 32, count // 32, norm_rows, 0)
    send(token_copy(2, h, 1))
    send(token_copy(1, h, 1))
    send(token_copy(2, h, 0))
    send_own(1)
    forward(0, 1)
    send_own(2)
    for d in range(2, deep):
        forward(0, d)
    token_copy(1, peers[1], 0).wait_recv()
    send(token_forward(2, 0))
    token_copy(2, peers[2], 1).wait_recv()
    send(token_forward(1, 1))
    for d in range(1, deep):
        forward(1, d)
    send_own(3)
    whole(0)
    whole(1)

    def heads_norm(raw, gain):
        parts = [per_head_norm(raw[:, i * HD : (i + 1) * HD], gain) for i in range(each)]
        return jnp.concatenate(parts, axis=1)

    def halo(j, side):
        tile = peers[j]
        rows = pl.ds(pl.multiple_of(tile * count, 16), count)
        left = jnp.where(c == 0, side, 1 - side)
        return remote(
            kv.at[1, :, rows], kv.at[2 * left, :, rows], kv_send.at[side, j], kv_recv.at[side, j],
            far if side else sibling,
        )

    def keys_of(j):
        tile = peers[j]
        rows = pl.ds(pl.multiple_of(tile * count, 16), count)
        left = mod[tile]
        kv[1, 0, rows, :] = heads_norm(add_rows(left, wbuf[0]), k_gain[...])
        kv[1, 1, rows, :] = add_rows(left, wbuf[1]).astype(jnp.bfloat16)
        send(halo(j, 0))

    def queries_of(t):
        rows = pl.ds(t * count, count)
        query[rows, :] = heads_norm(add_rows(mod[t], wbuf[2]), q_gain[...])

    keys_of(0)
    forward(2, 1)
    token_copy(1, peers[1], 1).wait_recv()
    keys_of(1)
    if deep > 2:
        forward(2, 2)
    send(halo(0, 1), has_far)
    send(halo(1, 1), has_far)
    token_copy(2, peers[2], 0).wait_recv()
    keys_of(2)
    send(halo(2, 1), has_far)
    token_forward(1, 0).wait_recv()
    token_forward(1, 1).wait_recv()
    keys_of(3)
    for d in range(3, deep):
        forward(2, d)
    forward(3, 1)
    send(halo(3, 1), has_far)
    whole(2)
    queries_of(0)
    queries_of(1)
    if deep > 2:
        forward(3, 2)
    queries_of(2)
    queries_of(3)
    tiles = len(peers)

    def attend(place, t, first):
        low, high = max(t - 1, 0), min(t + 2, tiles)
        rows = pl.ds(low * count, (high - low) * count)

        for i in range(each):
            columns = pl.ds(i * HD, HD)
            state = None
            if not first:
                state = (tops[i, t, :, :1], totals[i, t, :, :1], sums[i, t])
            top, total, summed = softmax_step(
                state,
                query[pl.ds(t * count, count), columns],
                kv[place, 0, rows, columns],
                kv[place, 1, rows, columns],
            )
            tops[i, t] = jnp.broadcast_to(top, (count, HD))
            totals[i, t] = jnp.broadcast_to(total, (count, HD))
            sums[i, t] = summed

    def out_forward(peer, part):
        first, size = (0, deep // 2) if part == 0 else (deep // 2, deep - deep // 2)
        block = obuf.at[peers[3 - peer], pl.ds(first, size), c]
        return remote(block, block, of_send.at[part], of_recv.at[part], (peers[peer], w))

    def out_sibling(j, core):
        block = obuf.at[peers[j], :, core]
        return remote(block, block, os_send.at[j], os_recv.at[j], sibling)

    for t in range(tiles):
        attend(1, t, True)
        if t == 2:
            for d in range(3, deep):
                forward(3, d)
    for j in range(tiles):
        halo(j, 0).wait_recv()
    for t in range(tiles):
        attend(2 - 2 * c, t, False)
        if t == 1:
            for j in (1, 2):
                for layer in range(deep):
                    block = obuf.at[peers[j], layer, c]
                    remote(
                        block, block, o_send.at[j, layer], o_recv.at[j, layer], (peers[j], w)
                    ).wait_recv()
                send(out_forward(3 - j, j - 1))
            for j in (1, 2):
                send(out_sibling(j, c))
    for j in range(tiles):
        pl.when(has_far)(halo(j, 1).wait_recv)

    def attended_copy(tile, source, slot):
        rows = pl.ds(pl.multiple_of(tile * count, 16), count)
        columns = pl.ds(pl.multiple_of(source * mine, HD), mine)
        return remote(
            attended.at[rows], gathered.at[:, columns], a_send.at[slot], a_recv.at[source], (tile, w)
        )

    for t in range(tiles):
        pl.when(has_far)(lambda: attend(2 * c, t, False))
        parts = [(sums[i, t] / totals[i, t]).astype(jnp.bfloat16) for i in range(each)]
        block = jnp.concatenate(parts, axis=1)
        attended[pl.ds(t * count, count), :] = block
        send(attended_copy(t, h, t), h != t)

        def keep():
            gathered[:, pl.ds(pl.multiple_of(h * mine, HD), mine)] = block

        pl.when(h == t)(keep)

    for part in range(2):
        out_forward(2 - part, part).wait_recv()
    send(out_sibling(3, c))
    whole(3)
    for s in range(tiles):
        pl.when(h != s)(attended_copy(h, s, s).wait_recv)
    for j in range(1, tiles):
        out_sibling(j, 1 - c).wait_recv()
    for q in range(tiles):
        columns = slice(q * mine, (q + 1) * mine)
        product = add_rows(gathered[...], obuf[q].reshape(inner, mine))
        update[:, columns] = (gate[columns] * product).astype(jnp.bfloat16)
    for copy, cond in pending:
        if cond is None:
            copy.wait_send()
        else:
            pl.when(cond)(copy.wait_send)


def shards_heads(tokens, shift, scale, gate, qkv_weight, out_weight, q_gain, k_gain):
    tall, wide = lax.axis_size("ha"), lax.axis_size("wa")
    each = HEADS // tall
    inner, mine = HEADS * HD, HEADS // tall * HD
    width = tokens.shape[-1]
    flat = tokens.reshape(-1, width)
    count = flat.shape[0]
    vmem = pl.BlockSpec(memory_space=pltpu.VMEM)
    hbm = pl.BlockSpec(memory_space=pl.ANY)
    dma = pltpu.SemaphoreType.DMA
    state = pltpu.VMEM((each, tall, count, HD), jnp.float32)
    update = pl.pallas_call(
        lambda *refs: block_kernel(wide, *refs),
        out_shape=jax.ShapeDtypeStruct((count, width), jnp.bfloat16),
        in_specs=[vmem, vmem, vmem, vmem, hbm, hbm, vmem, vmem],
        out_specs=vmem,
        scratch_shapes=[
            pltpu.VMEM((tall, count, width), jnp.bfloat16),
            pltpu.VMEM((3, width, mine), jnp.bfloat16),
            pltpu.VMEM((tall, wide // 2, 2, inner // wide, mine), jnp.bfloat16),
            pltpu.VMEM((tall * count, mine), jnp.bfloat16),
            pltpu.VMEM((3, 2, tall * count, mine), jnp.bfloat16),
            pltpu.VMEM((tall * count, mine), jnp.bfloat16),
            pltpu.VMEM((count, inner), jnp.bfloat16),
            state,
            state,
            state,
            dma((4,)),
            dma((4, wide, 3)),
            dma((4, wide)),
            dma((3, 2)),
            dma((4, 2)),
            dma((2,)),
            dma((2, tall)),
            dma((2, tall)),
            dma((3, wide // 2)),
            dma((3, wide // 2)),
            dma((2,)),
            dma((2,)),
            dma((tall,)),
            dma((tall,)),
            dma((tall,)),
            dma((tall,)),
        ],
        compiler_params=pltpu.CompilerParams(
            collective_id=0, has_side_effects=True, vmem_limit_bytes=56 * 2**20
        ),
        cost_estimate=pl.CostEstimate(
            flops=9 * 10**9, bytes_accessed=4 * 10**6, transcendentals=6 * 10**6
        ),
        name="block",
    )(flat, shift, scale, gate, qkv_weight, out_weight, q_gain, k_gain)
    return update.reshape(tokens.shape)


def shards(tokens, *rest):
    plain = lax.axis_size("ha") != 4 or lax.axis_size("wa") % 2 or tokens.shape[0] != TILE_T
    return (shards_general if plain else shards_heads)(tokens, *rest)


def solution(mesh):
    return jax.shard_map(
        shards,
        mesh=mesh,
        in_specs=(P(None, "ha", "wa", None), P(), P(), P(), P("wa", None), P("wa", None), P(), P()),
        out_specs=P(None, "ha", "wa", None),
        check_vma=False,
    )
```
